256 devices in a mesh: row: 16 (over x_hi, z), col: 4 (over y), depth: 4 (over x_lo, core).
Axes of the slice: x: 4 (x_hi: 2, x_lo: 2; x = x_hi * 2 + x_lo), y: 4, z: 8, core: 2. Of those that a mesh axis runs over, the one named last changes fastest.
Arguments:
- basis: bfloat16 [4, 512, 65536], P('depth', 'row', 'col'), may hold values from -0.1875 to 0.1875
- targets: bfloat16 [4, 512, 4096], P('depth', 'col', 'row'), may hold values from -6 to 6
Outputs:
- cross: float32 [65536, 4096], P(('col', 'depth'), 'row')
The draws below stay inside these ranges and needn't reach their ends.
All inputs are finite; a program needn't handle non-finite values.
Results may differ from the reference program's by a relative error of at most 0.0003.
Values may be sent and summed in bfloat16 or wider, within the bound.
A program may use at most 128 MiB of HBM per device.

```python
import jax
import jax.numpy as jnp
from jax import lax

K = 65536
O = 4096
SPD = 512
SAMPLES = 2048
N_DEPTH = 4


def with_spikes(array, rng, source, target, shards_of, factor):
    owner, partner = [(jnp.arange(array.shape[axis_at]) // (array.shape[axis_at] // shards_of)).reshape([-1 if axis == axis_at else 1 for axis in range(array.ndim)]) for axis_at in (source, target)]
    chosen = jax.random.permutation(rng, shards_of)[partner]
    strong = (owner == chosen) | (owner == (partner + shards_of // 2) % shards_of)
    return jnp.where(strong, factor * array, array)


def levels(stream_key, shape, split, least, largest):
    factor_of = 1.0
    for dim, parts in split:
        draws = jax.random.uniform(jax.random.fold_in(jax.random.fold_in(stream_key, 6), dim), (parts,), jnp.float32, least / len(split), largest / len(split))
        factor_of = factor_of * jnp.repeat(jnp.exp(draws), shape[dim] // parts).reshape((-1,) + (1,) * (len(shape) - 1 - dim))
    return factor_of


def centred(key, shape, spread, reach, split=(), held_as=jnp.bfloat16):
    array = spread * jax.random.normal(key, shape, jnp.float32)
    if split:
        array = array * levels(key, shape, split, -0.22, 0.18)
    return jnp.clip(array, -reach, reach).astype(held_as)


def gaussian_with(rng, shape, spread, bound, pieces, heavy, kind=jnp.bfloat16):
    array = spread * jax.random.normal(rng, shape, jnp.float32)
    if pieces:
        array = array * levels(rng, shape, pieces, -0.22, 0.18)
    return jnp.clip(with_spikes(array, jax.random.fold_in(rng, 3), *heavy), -bound, bound).astype(kind)


def setup_inputs(seed: int = 0) -> dict:
    arg_keys = jax.random.split(jax.random.key(seed), 3)
    return {
        "basis": gaussian_with(arg_keys[0], (N_DEPTH, SPD, K), SAMPLES ** -0.5, 0.1875, ((0, 4), (1, 16), (2, 4)), (0, 2, 4, 2.0)),
        "targets": centred(arg_keys[1], (N_DEPTH, SPD, O), 1.0, 6.0, ((0, 4), (1, 4), (2, 16))),
    }


def reference(basis, targets):
    def layer_term(total, pair):
        layer_basis = pair[0].astype(jnp.float32)
        layer_target = pair[1].astype(jnp.float32)
        partial_value = jnp.dot(layer_basis.T, layer_target, preferred_element_type=jnp.float32, precision=lax.Precision.HIGHEST)
        return total + partial_value, None

    start_total = jnp.zeros((basis.shape[2], targets.shape[2]), jnp.float32)
    cross, unused = lax.scan(layer_term, start_total, (basis, targets))
    return cross
```

```python
import jax
import jax.numpy as jnp
from jax import lax
from jax.experimental import pallas as pl
from jax.experimental.pallas import tpu as pltpu
from jax.sharding import PartitionSpec as P

MESH = pl.DeviceIdType.MESH
NZ = 8
NX = 8
CHUNKS = 8
GROUP = 2


def kernel(
    basis, targets, out, gath, tg, ob,
    x_send, x_recv, z_send, z_recv, t_send, t_recv, o_send, o_recv,
):
    tile = gath.shape[0] * gath.shape[2]
    kc = gath.shape[2]
    rows = basis.shape[0]
    piece = NX * rows
    half = piece // 2
    row, y, d = (lax.axis_index(a) for a in ("row", "col", "depth"))
    hi, z = row // NZ, row % NZ
    me = hi * 4 + d
    up, down = (z + 1) % NZ, (z + NZ - 1) % NZ

    def x_peer(idx):
        return ((idx // 4) * NZ + z, y, idx % 4)

    def z_peer(zz):
        return (hi * NZ + zz, y, d)

    def y_peer(yy):
        return (row, yy, d)

    barrier = pltpu.get_barrier_semaphore()
    for i in range(1, NX):
        pl.semaphore_signal(barrier, inc=1, device_id=x_peer((me + i) % NX), device_id_type=MESH)
    for zz in (up, down):
        pl.semaphore_signal(barrier, inc=1, device_id=z_peer(zz), device_id_type=MESH)
    for i in range(1, 4):
        pl.semaphore_signal(barrier, inc=1, device_id=y_peer((y + i) % 4), device_id_type=MESH)
    pl.semaphore_wait(barrier, NX - 1 + 2 + 3)

    def columns(idx, c):
        owner = (1 - (idx % 4) // 2) * 2 + idx % 2
        start = owner * 2 * tile + (idx // 4) * tile + c * kc
        return pl.ds(pl.multiple_of(start, kc), kc)

    def scatter_basis(c):
        mine = gath.at[c, pl.ds(pl.multiple_of(z * piece + me * rows, rows), rows), :]
        for i in range(1, NX):
            idx = (me + i) % NX
            pltpu.make_async_remote_copy(
                basis.at[:, columns(idx, c)], mine, x_send, x_recv.at[c],
                device_id=x_peer(idx), device_id_type=MESH,
            ).start()
        pltpu.make_async_copy(basis.at[:, columns(me, c)], mine, x_recv.at[c]).start()

    def origin(c, zz, first=0, count=piece):
        return gath.at[c, pl.ds(pl.multiple_of(zz * piece + first, half), count), :]

    def wait_bytes(ref, sem):
        pltpu.make_async_copy(ref, ref, sem).wait()

    def part(way, hop):
        if hop < 3:
            return 0, piece
        return (0, half) if way == 0 else (half, half)

    def z_origin(way, hop):
        return (z - hop + NZ) % NZ if way == 0 else (z + hop) % NZ

    def z_copy(c, way, hop):
        ref = origin(c, z_origin(way, hop), *part(way, hop))
        return pltpu.make_async_remote_copy(
            ref, ref, z_send.at[way], z_recv.at[way, c, hop],
            device_id=z_peer(up if way == 0 else down), device_id_type=MESH,
        )

    def z_wait(c, way, hop):
        ref = origin(c, z_origin(way, hop + 1), *part(way, hop))
        wait_bytes(ref, z_recv.at[way, c, hop])

    def t_region(yy):
        return tg.at[:, pl.ds((yy % 2) * 4, 4), pl.ds((yy // 2) * 4, 4), :, :]

    def t_own():
        return tg.at[hi, pl.ds((y % 2) * 4, 4), (y // 2) * 4 + d, :, :]

    def gather_targets_x():
        for i in range(1, NX):
            pltpu.make_async_remote_copy(
                targets, t_own(), t_send.at[0], t_recv.at[0],
                device_id=x_peer((me + i) % NX), device_id_type=MESH,
            ).start()
        pltpu.make_async_copy(targets, t_own(), t_recv.at[0]).start()

    def gather_targets_y():
        wait_bytes(t_region(y), t_recv.at[0])
        for i in (2, 1, 3):
            pltpu.make_async_remote_copy(
                t_region(y), t_region(y), t_send.at[1], t_recv.at[1],
                device_id=y_peer((y + i) % 4), device_id_type=MESH,
            ).start()

    def multiply(c):
        a = gath[c]
        for h in range(2):
            ob[c, h] = lax.dot_general(
                a, tg[h].reshape(NZ * piece, tg.shape[4]),
                (((0,), (0,)), ((), ())), preferred_element_type=jnp.float32,
            )
            lo = 1 - d // 2
            pltpu.make_async_remote_copy(
                ob.at[c, h], out.at[pl.ds(pl.multiple_of(hi * tile + c * kc, kc), kc), :],
                o_send, o_recv,
                device_id=(h * NZ + z, y, lo * 2 + d % 2), device_id_type=MESH,
            ).start()

    groups = CHUNKS // GROUP

    for j in range(GROUP):
        scatter_basis(j)
    gather_targets_x()

    def step(g, carry):
        for hop in range(4):
            for j in range(GROUP):
                c = g * GROUP + j
                if hop == 0:
                    wait_bytes(origin(c, z), x_recv.at[c])
                for way in range(2):
                    if hop > 0:
                        z_wait(c, way, hop - 1)
                    z_copy(c, way, hop).start()
            if hop == 0:
                pl.when(g == 0)(gather_targets_y)

                @pl.when(g < groups - 1)
                def _():
                    for j in range(GROUP):
                        scatter_basis((g + 1) * GROUP + j)

            if hop == 1:
                @pl.when(g > 0)
                def _():
                    @pl.when(g == 1)
                    def _():
                        wait_bytes(tg.at[:, pl.ds(0, 6)], t_recv.at[1])

                    for j in range(GROUP):
                        c = (g - 1) * GROUP + j
                        for way in range(2):
                            z_wait(c, way, 3)
                        multiply(c)
        return carry

    lax.fori_loop(0, groups, step, 0)
    for j in range(GROUP):
        c = CHUNKS - GROUP + j
        for way in range(2):
            z_wait(c, way, 3)
        multiply(c)

    wait_bytes(gath.at[:, pl.ds(0, (NX - 1) * rows), :], x_send)
    for way in range(2):
        wait_bytes(gath.at[:, pl.ds(0, 3 * piece + half), :], z_send.at[way])
    wait_bytes(tg.at[0, pl.ds(0, 4), pl.ds(0, NX - 1)], t_send.at[0])
    wait_bytes(tg.at[:, pl.ds(0, 6)], t_send.at[1])
    wait_bytes(ob, o_send)
    wait_bytes(out, o_recv)


def per_device(basis, targets):
    rows, columns = basis.shape[1:]
    samples, outs = targets.shape[1:]
    tile = columns // NX
    kc = tile // CHUNKS
    return pl.pallas_call(
        kernel,
        out_shape=jax.ShapeDtypeStruct((2 * tile, outs), jnp.float32),
        in_specs=[pl.BlockSpec(memory_space=pl.ANY)] * 2,
        out_specs=pl.BlockSpec(memory_space=pl.ANY),
        scratch_shapes=[
            pltpu.VMEM((CHUNKS, NZ * NX * rows, kc), jnp.bfloat16),
            pltpu.VMEM((2, NZ, NX, rows, outs), jnp.bfloat16),
            pltpu.VMEM((CHUNKS, 2, kc, outs), jnp.float32),
            pltpu.SemaphoreType.DMA,
            pltpu.SemaphoreType.DMA((CHUNKS,)),
            pltpu.SemaphoreType.DMA((2,)),
            pltpu.SemaphoreType.DMA((2, CHUNKS, 4)),
            pltpu.SemaphoreType.DMA((2,)),
            pltpu.SemaphoreType.DMA((2,)),
            pltpu.SemaphoreType.DMA,
            pltpu.SemaphoreType.DMA,
        ],
        compiler_params=pltpu.CompilerParams(
            collective_id=1, has_side_effects=True, vmem_limit_bytes=48 * 2**20
        ),
        name="cross",
    )(basis.reshape(rows, columns), targets.reshape(samples // rows, rows, outs))


def solution(mesh):
    in_specs = (P("depth", "row", "col"), P("depth", "col", "row"))
    out_specs = P(("col", "depth"), "row")
    return jax.shard_map(
        per_device, mesh=mesh, in_specs=in_specs, out_specs=out_specs, check_vma=False
    )
```

```python
import jax
import jax.numpy as jnp
from jax import lax
from jax.experimental import pallas as pl
from jax.experimental.pallas import tpu as pltpu
from jax.sharding import PartitionSpec as P

MESH = pl.DeviceIdType.MESH
NZ = 8
NX = 8
CHUNKS = 16
WHEN = (0, 2, 4, 6, 8)
AHEAD = 3
PRIO_Z, PRIO_X, PRIO_O = 0, 0, 0
LOCAL = -1


def kernel(
    basis, targets, out, gath, tg, ob,
    own_sem, x_send, x_recv, z_send, z_recv, t_send, t_recv, o_send, o_recv,
):
    kc = gath.shape[2]
    tile = CHUNKS * kc
    rows = basis.shape[0]
    block = NX * rows
    row, y, d = (lax.axis_index(a) for a in ("row", "col", "depth"))
    hi, z = row // NZ, row % NZ
    lo, core = d // 2, d % 2
    up, down = (z + 1) % NZ, (z + NZ - 1) % NZ

    def flip(bit, i):
        return 1 - bit if i else bit

    def x_peer(i):
        return flip(hi, i & 4), flip(lo, i & 2), flip(core, i & 1)

    def x_device(i):
        h, l, k = x_peer(i)
        return (h * NZ + z, y, l * 2 + k)

    def z_device(way):
        return (hi * NZ + (up if way == 0 else down), y, d)

    def y_device(i):
        return (row, (y + i) % 4, d)

    def columns(i, c):
        h, l, k = x_peer(i)
        start = ((1 - l) * 2 + k) * 2 * tile + h * tile + c * kc
        return pl.ds(pl.multiple_of(start, kc), kc)

    def rows_of(zz, first, count):
        return pl.ds(pl.multiple_of(zz * block + first, 16), count)

    def wait_bytes(ref, sem):
        pltpu.make_async_copy(ref, ref, sem).wait()

    for c in range(CHUNKS):
        pltpu.make_async_copy(
            basis.at[:, columns(0, c)], gath.at[c, rows_of(z, 0, rows), :], own_sem
        ).start()

    barrier = pltpu.get_barrier_semaphore()
    friends = [x_device(i) for i in range(1, NX)] + [z_device(0), z_device(1)]
    friends += [y_device(i) for i in range(1, 4)]
    for friend in friends:
        pl.semaphore_signal(barrier, inc=1, device_id=friend, device_id_type=MESH)
    pl.semaphore_wait(barrier, len(friends))

    def scatter_basis(c):
        for i in range(1, NX):
            pltpu.make_async_remote_copy(
                basis.at[:, columns(i, c)], gath.at[c, rows_of(z, i * rows, rows), :],
                x_send, x_recv.at[c], device_id=x_device(i), device_id_type=MESH,
            ).start(priority=PRIO_X)

    def z_part(c, zz, way, hop):
        local = isinstance(c, int)
        first, count = (0, rows) if local else (rows, block - rows)
        if hop == 3:
            count //= 2
            first += way * count
        if local:
            return gath.at[:, rows_of(zz, first, count), :]
        return gath.at[c, rows_of(zz, first, count), :]

    def z_origin(way, hop):
        return (z - hop + NZ) % NZ if way == 0 else (z + hop) % NZ

    def z_send_hop(c, way, hop):
        ref = z_part(c, z_origin(way, hop), way, hop)
        pltpu.make_async_remote_copy(
            ref, ref, z_send.at[way], z_recv.at[way, c + 1, hop],
            device_id=z_device(way), device_id_type=MESH,
        ).start(priority=PRIO_Z)

    def z_wait(c, way, hop):
        wait_bytes(z_part(c, z_origin(way, hop + 1), way, hop), z_recv.at[way, c + 1, hop])

    def t_region(yy):
        half = yy // 2 + hi - 2 * (yy // 2) * hi
        return tg.at[:, pl.ds((yy % 2) * 4, 4), pl.ds(half * 4, 4), :, :]

    def t_block(i):
        h = x_peer(i)[0]
        half = y // 2 + h - 2 * (y // 2) * h
        return tg.at[hi, pl.ds((y % 2) * 4, 4), half * 4 + i % 4, :, :]

    def gather_targets_x():
        for i in range(1, NX):
            pltpu.make_async_remote_copy(
                targets, t_block(i), t_send.at[0], t_recv.at[0],
                device_id=x_device(i), device_id_type=MESH,
            ).start(priority=PRIO_X)
        pltpu.make_async_copy(targets, t_block(0), t_recv.at[0]).start()

    def gather_targets_y():
        wait_bytes(t_region(y), t_recv.at[0])
        for i in (2, 1, 3):
            pltpu.make_async_remote_copy(
                t_region(y), t_region(y), t_send.at[1], t_recv.at[1],
                device_id=y_device(i), device_id_type=MESH,
            ).start(priority=PRIO_X)

    def multiply(c):
        a = gath[c]
        for h in range(2):
            ob[c, h] = lax.dot_general(
                a, tg[h].reshape(NZ * block, tg.shape[4]),
                (((0,), (0,)), ((), ())), preferred_element_type=jnp.float32,
            )
            pltpu.make_async_remote_copy(
                ob.at[c, h], out.at[pl.ds(pl.multiple_of(hi * tile + c * kc, kc), kc), :],
                o_send, o_recv,
                device_id=(h * NZ + z, y, (1 - lo) * 2 + core), device_id_type=MESH,
            ).start(priority=PRIO_O)

    def forward(c, hop):
        for way in range(2):
            if hop:
                z_wait(c, way, hop - 1)
            z_send_hop(c, way, hop)

    wait_bytes(gath.at[:, rows_of(z, 0, rows), :], own_sem)
    forward(LOCAL, 0)
    for c in range(AHEAD):
        scatter_basis(c)
    gather_targets_x()

    def step(t, carry):
        for hop in (3, 2, 1):
            c = t - WHEN[hop]
            pl.when(c == LOCAL)(lambda: forward(LOCAL, hop))
            pl.when((c >= 0) & (c < CHUNKS))(lambda: forward(c, hop))

        @pl.when(t < CHUNKS)
        def _():
            wait_bytes(gath.at[t, rows_of(z, rows, block - rows), :], x_recv.at[t])
            forward(t, 0)

        pl.when(t == 1)(gather_targets_y)

        @pl.when(t + AHEAD < CHUNKS)
        def _():
            scatter_basis(t + AHEAD)

        c = t - WHEN[4]

        @pl.when(c == LOCAL)
        def _():
            for way in range(2):
                z_wait(LOCAL, way, 3)
            wait_bytes(tg.at[:, pl.ds(0, 6)], t_recv.at[1])

        @pl.when(c >= 0)
        def _():
            for way in range(2):
                z_wait(c, way, 3)
            multiply(c)

        return carry

    lax.fori_loop(0, CHUNKS + WHEN[4], step, 0)

    wait_bytes(gath.at[:, pl.ds(0, block - rows), :], x_send)
    for way in range(2):
        wait_bytes(gath.at[:, pl.ds(0, 3 * block + block // 2), :], z_send.at[way])
    wait_bytes(tg.at[0, pl.ds(0, 4), pl.ds(0, NX - 1)], t_send.at[0])
    wait_bytes(tg.at[:, pl.ds(0, 6)], t_send.at[1])
    wait_bytes(ob, o_send)
    wait_bytes(out, o_recv)


def per_device(basis, targets):
    rows, columns = basis.shape[1:]
    samples, outs = targets.shape[1:]
    tile = columns // NX
    kc = tile // CHUNKS
    return pl.pallas_call(
        kernel,
        out_shape=jax.ShapeDtypeStruct((2 * tile, outs), jnp.float32),
        in_specs=[pl.BlockSpec(memory_space=pl.ANY)] * 2,
        out_specs=pl.BlockSpec(memory_space=pl.ANY),
        scratch_shapes=[
            pltpu.VMEM((CHUNKS, NZ * NX * rows, kc), jnp.bfloat16),
            pltpu.VMEM((2, NZ, NX, rows, outs), jnp.bfloat16),
            pltpu.VMEM((CHUNKS, 2, kc, outs), jnp.float32),
            pltpu.SemaphoreType.DMA,
            pltpu.SemaphoreType.DMA,
            pltpu.SemaphoreType.DMA((CHUNKS,)),
            pltpu.SemaphoreType.DMA((2,)),
            pltpu.SemaphoreType.DMA((2, CHUNKS + 1, 4)),
            pltpu.SemaphoreType.DMA((2,)),
            pltpu.SemaphoreType.DMA((2,)),
            pltpu.SemaphoreType.DMA,
            pltpu.SemaphoreType.DMA,
        ],
        compiler_params=pltpu.CompilerParams(
            collective_id=1, has_side_effects=True, vmem_limit_bytes=48 * 2**20
        ),
        name="cross",
    )(
        pltpu.with_memory_space_constraint(basis.reshape(rows, columns), pltpu.HBM),
        pltpu.with_memory_space_constraint(
            targets.reshape(samples // rows, rows, outs), pltpu.HBM
        ),
    )


def solution(mesh):
    in_specs = (P("depth", "row", "col"), P("depth", "col", "row"))
    out_specs = P(("col", "depth"), "row")
    return jax.shard_map(
        per_device, mesh=mesh, in_specs=in_specs, out_specs=out_specs, check_vma=False
    )
```

```python
import jax
import jax.numpy as jnp
from jax import lax
from jax.experimental import pallas as pl
from jax.experimental.pallas import tpu as pltpu
from jax.sharding import PartitionSpec as P

MESH = pl.DeviceIdType.MESH
NZ = 8
NX = 8
CHUNKS = 16
WHEN = (0, 2, 4, 6, 8)
AHEAD = 3
WAVES = 2


def kernel(
    basis, targets, out, gath, tg, ob,
    own_sem, e_recv, x_send, x_recv, z_send, z_recv, t_send, t_recv, o_send, o_recv,
):
    kc = gath.shape[2]
    tile = CHUNKS * kc
    rows = basis.shape[0]
    block = NX * rows
    row, y, d = (lax.axis_index(a) for a in ("row", "col", "depth"))
    hi, z = row // NZ, row % NZ
    lo, core = d // 2, d % 2
    up, down = (z + 1) % NZ, (z + NZ - 1) % NZ

    def flip(bit, i):
        return 1 - bit if i else bit

    def x_peer(i):
        return flip(hi, i & 4), flip(lo, i & 2), flip(core, i & 1)

    def x_device(i):
        h, l, k = x_peer(i)
        return (h * NZ + z, y, l * 2 + k)

    def z_device(way):
        return (hi * NZ + (up if way == 0 else down), y, d)

    def y_device(i):
        return (row, (y + i) % 4, d)

    def columns(i, c):
        h, l, k = x_peer(i)
        start = ((1 - l) * 2 + k) * 2 * tile + h * tile + c * kc
        return pl.ds(pl.multiple_of(start, kc), kc)

    def rows_of(zz, first, count):
        return pl.ds(pl.multiple_of(zz * block + first, 16), count)

    def wait_bytes(ref, sem):
        pltpu.make_async_copy(ref, ref, sem).wait()

    for c in range(CHUNKS):
        pltpu.make_async_copy(
            basis.at[:, columns(0, c)], gath.at[c, rows_of(z, 0, rows), :], own_sem
        ).start()

    barrier = pltpu.get_barrier_semaphore()
    friends = [x_device(i) for i in range(1, NX)] + [z_device(0), z_device(1)]
    friends += [y_device(i) for i in range(1, 4)]
    for friend in friends:
        pl.semaphore_signal(barrier, inc=1, device_id=friend, device_id_type=MESH)
    pl.semaphore_wait(barrier, len(friends))

    def scatter_basis(c):
        for i in range(WAVES, NX):
            pltpu.make_async_remote_copy(
                basis.at[:, columns(i, c)], gath.at[c, rows_of(z, i * rows, rows), :],
                x_send, x_recv.at[c], device_id=x_device(i), device_id_type=MESH,
            ).start()

    def scatter_early():
        for i in range(1, WAVES):
            for c in range(CHUNKS):
                pltpu.make_async_remote_copy(
                    basis.at[:, columns(i, c)], gath.at[c, rows_of(z, i * rows, rows), :],
                    x_send, e_recv.at[i], device_id=x_device(i), device_id_type=MESH,
                ).start()

    def z_part(c, zz, way, hop):
        local = isinstance(c, int)
        first, count = WAVES * rows, block - WAVES * rows
        if local:
            first, count = (c + WAVES) * rows, rows
        if hop == 3:
            count //= 2
            first += way * count
        if local:
            return gath.at[:, rows_of(zz, first, count), :]
        return gath.at[c, rows_of(zz, first, count), :]

    def z_origin(way, hop):
        return (z - hop + NZ) % NZ if way == 0 else (z + hop) % NZ

    def z_send_hop(c, way, hop):
        ref = z_part(c, z_origin(way, hop), way, hop)
        pltpu.make_async_remote_copy(
            ref, ref, z_send.at[way], z_recv.at[way, c + WAVES, hop],
            device_id=z_device(way), device_id_type=MESH,
        ).start()

    def z_wait(c, way, hop):
        wait_bytes(z_part(c, z_origin(way, hop + 1), way, hop), z_recv.at[way, c + WAVES, hop])

    def t_region(yy):
        half = yy // 2 + hi - 2 * (yy // 2) * hi
        return tg.at[:, pl.ds((yy % 2) * 4, 4), pl.ds(half * 4, 4), :, :]

    def t_block(i):
        h = x_peer(i)[0]
        half = y // 2 + h - 2 * (y // 2) * h
        return tg.at[hi, pl.ds((y % 2) * 4, 4), half * 4 + i % 4, :, :]

    def gather_targets_x():
        for i in range(1, NX):
            pltpu.make_async_remote_copy(
                targets, t_block(i), t_send.at[0], t_recv.at[0],
                device_id=x_device(i), device_id_type=MESH,
            ).start()
        pltpu.make_async_copy(targets, t_block(0), t_recv.at[0]).start()

    def gather_targets_y():
        wait_bytes(t_region(y), t_recv.at[0])
        for i in (2, 1, 3):
            pltpu.make_async_remote_copy(
                t_region(y), t_region(y), t_send.at[1], t_recv.at[1],
                device_id=y_device(i), device_id_type=MESH,
            ).start()

    def multiply(c):
        a = gath[c]
        for h in range(2):
            ob[c, h] = lax.dot_general(
                a, tg[h].reshape(NZ * block, tg.shape[4]),
                (((0,), (0,)), ((), ())), preferred_element_type=jnp.float32,
            )
            pltpu.make_async_remote_copy(
                ob.at[c, h], out.at[pl.ds(pl.multiple_of(hi * tile + c * kc, kc), kc), :],
                o_send, o_recv,
                device_id=(h * NZ + z, y, (1 - lo) * 2 + core), device_id_type=MESH,
            ).start()

    def forward(c, hop):
        for way in range(2):
            if hop:
                z_wait(c, way, hop - 1)
            z_send_hop(c, way, hop)

    wait_bytes(gath.at[:, rows_of(z, 0, rows), :], own_sem)
    forward(-WAVES, 0)
    scatter_early()
    for c in range(AHEAD):
        scatter_basis(c)
    for i in range(1, WAVES):
        wait_bytes(gath.at[:, rows_of(z, i * rows, rows), :], e_recv.at[i])
        forward(i - WAVES, 0)
    gather_targets_x()

    def step(t, carry):
        @pl.when(t < CHUNKS)
        def _():
            wait_bytes(gath.at[t, rows_of(z, WAVES * rows, block - WAVES * rows), :], x_recv.at[t])
            forward(t, 0)

        for hop in (1, 2, 3):
            c = t - WHEN[hop]
            for wave in range(-WAVES, 0):
                pl.when(c == wave)(lambda: forward(wave, hop))
            pl.when((c >= 0) & (c < CHUNKS))(lambda: forward(c, hop))

        pl.when(t == 1)(gather_targets_y)

        @pl.when(t + AHEAD < CHUNKS)
        def _():
            scatter_basis(t + AHEAD)

        c = t - WHEN[4]

        @pl.when(c == -1)
        def _():
            for way in range(2):
                for wave in range(-WAVES, 0):
                    z_wait(wave, way, 3)
            wait_bytes(tg.at[:, pl.ds(0, 6)], t_recv.at[1])

        @pl.when(c >= 0)
        def _():
            for way in range(2):
                z_wait(c, way, 3)
            multiply(c)

        return carry

    lax.fori_loop(0, CHUNKS + WHEN[4], step, 0)

    wait_bytes(gath.at[:, pl.ds(0, block - rows), :], x_send)
    for way in range(2):
        wait_bytes(gath.at[:, pl.ds(0, 3 * block + block // 2), :], z_send.at[way])
    wait_bytes(tg.at[0, pl.ds(0, 4), pl.ds(0, NX - 1)], t_send.at[0])
    wait_bytes(tg.at[:, pl.ds(0, 6)], t_send.at[1])
    wait_bytes(ob, o_send)
    wait_bytes(out, o_recv)


def per_device(basis, targets):
    rows, columns = basis.shape[1:]
    samples, outs = targets.shape[1:]
    tile = columns // NX
    kc = tile // CHUNKS
    return pl.pallas_call(
        kernel,
        out_shape=jax.ShapeDtypeStruct((2 * tile, outs), jnp.float32),
        in_specs=[pl.BlockSpec(memory_space=pl.ANY)] * 2,
        out_specs=pl.BlockSpec(memory_space=pl.ANY),
        scratch_shapes=[
            pltpu.VMEM((CHUNKS, NZ * NX * rows, kc), jnp.bfloat16),
            pltpu.VMEM((2, NZ, NX, rows, outs), jnp.bfloat16),
            pltpu.VMEM((CHUNKS, 2, kc, outs), jnp.float32),
            pltpu.SemaphoreType.DMA,
            pltpu.SemaphoreType.DMA((WAVES,)),
            pltpu.SemaphoreType.DMA,
            pltpu.SemaphoreType.DMA((CHUNKS,)),
            pltpu.SemaphoreType.DMA((2,)),
            pltpu.SemaphoreType.DMA((2, CHUNKS + WAVES, 4)),
            pltpu.SemaphoreType.DMA((2,)),
            pltpu.SemaphoreType.DMA((2,)),
            pltpu.SemaphoreType.DMA,
            pltpu.SemaphoreType.DMA,
        ],
        compiler_params=pltpu.CompilerParams(
            collective_id=1, has_side_effects=True, vmem_limit_bytes=48 * 2**20
        ),
        name="cross",
    )(
        pltpu.with_memory_space_constraint(basis.reshape(rows, columns), pltpu.HBM),
        pltpu.with_memory_space_constraint(
            targets.reshape(samples // rows, rows, outs), pltpu.HBM
        ),
    )


def solution(mesh):
    in_specs = (P("depth", "row", "col"), P("depth", "col", "row"))
    out_specs = P(("col", "depth"), "row")
    return jax.shard_map(
        per_device, mesh=mesh, in_specs=in_specs, out_specs=out_specs, check_vma=False
    )
```

```python
import jax
import jax.numpy as jnp
from jax import lax
from jax.experimental import pallas as pl
from jax.experimental.pallas import tpu as pltpu
from jax.sharding import PartitionSpec as P

MESH = pl.DeviceIdType.MESH
NZ = 8
NX = 8
CHUNKS = 16
WHEN = (0, 2, 4, 6, 8)
TAIL = CHUNKS + 1
AHEAD = 3
WAVES = 2


def kernel(
    basis, targets, out, gath, tg, ob,
    own_sem, e_recv, x_send, x_recv, z_send, z_recv, t_send, t_recv, o_send, o_recv,
):
    kc = gath.shape[2]
    tile = CHUNKS * kc
    rows = basis.shape[0]
    block = NX * rows
    row, y, d = (lax.axis_index(a) for a in ("row", "col", "depth"))
    hi, z = row // NZ, row % NZ
    lo, core = d // 2, d % 2
    up, down = (z + 1) % NZ, (z + NZ - 1) % NZ

    def flip(bit, i):
        return 1 - bit if i else bit

    def x_peer(i):
        return flip(hi, i & 4), flip(lo, i & 2), flip(core, i & 1)

    def x_device(i):
        h, l, k = x_peer(i)
        return (h * NZ + z, y, l * 2 + k)

    def z_device(way):
        return (hi * NZ + (up if way == 0 else down), y, d)

    def y_device(i):
        return (row, (y + i) % 4, d)

    def columns(i, c):
        h, l, k = x_peer(i)
        start = ((1 - l) * 2 + k) * 2 * tile + h * tile + c * kc
        return pl.ds(pl.multiple_of(start, kc), kc)

    def rows_of(zz, first, count):
        return pl.ds(pl.multiple_of(zz * block + first, 16), count)

    def wait_bytes(ref, sem):
        pltpu.make_async_copy(ref, ref, sem).wait()

    for c in range(CHUNKS):
        pltpu.make_async_copy(
            basis.at[:, columns(0, c)], gath.at[c, rows_of(z, 0, rows), :], own_sem
        ).start()

    barrier = pltpu.get_barrier_semaphore()
    friends = [x_device(i) for i in range(1, NX)] + [z_device(0), z_device(1)]
    friends += [y_device(i) for i in range(1, 4)]
    for friend in friends:
        pl.semaphore_signal(barrier, inc=1, device_id=friend, device_id_type=MESH)
    pl.semaphore_wait(barrier, len(friends))

    def scatter_basis(c):
        for i in range(WAVES, NX):
            pltpu.make_async_remote_copy(
                basis.at[:, columns(i, c)], gath.at[c, rows_of(z, i * rows, rows), :],
                x_send, x_recv.at[c], device_id=x_device(i), device_id_type=MESH,
            ).start()

    def scatter_early():
        for i in range(1, WAVES):
            for c in range(CHUNKS):
                pltpu.make_async_remote_copy(
                    basis.at[:, columns(i, c)], gath.at[c, rows_of(z, i * rows, rows), :],
                    x_send, e_recv.at[i], device_id=x_device(i), device_id_type=MESH,
                ).start()

    def z_part(c, zz, way, hop):
        local = isinstance(c, int)
        first, count = WAVES * rows, block - WAVES * rows
        if local:
            first, count = (c + WAVES) * rows, rows
        if hop == 3:
            count //= 2
            first += way * count
        if local:
            return gath.at[:, rows_of(zz, first, count), :]
        return gath.at[c, rows_of(zz, first, count), :]

    def z_origin(way, hop):
        return (z - hop + NZ) % NZ if way == 0 else (z + hop) % NZ

    def z_send_hop(c, way, hop):
        ref = z_part(c, z_origin(way, hop), way, hop)
        pltpu.make_async_remote_copy(
            ref, ref, z_send.at[way], z_recv.at[way, c + WAVES, hop],
            device_id=z_device(way), device_id_type=MESH,
        ).start()

    def z_wait(c, way, hop):
        wait_bytes(z_part(c, z_origin(way, hop + 1), way, hop), z_recv.at[way, c + WAVES, hop])

    def t_region(yy):
        half = yy // 2 + hi - 2 * (yy // 2) * hi
        return tg.at[:, pl.ds((yy % 2) * 4, 4), pl.ds(half * 4, 4), :, :]

    def t_block(i):
        h = x_peer(i)[0]
        half = y // 2 + h - 2 * (y // 2) * h
        return tg.at[hi, pl.ds((y % 2) * 4, 4), half * 4 + i % 4, :, :]

    def gather_targets_x():
        for i in range(1, NX):
            pltpu.make_async_remote_copy(
                targets, t_block(i), t_send.at[0], t_recv.at[0],
                device_id=x_device(i), device_id_type=MESH,
            ).start()
        pltpu.make_async_copy(targets, t_block(0), t_recv.at[0]).start()

    def gather_targets_y():
        wait_bytes(t_region(y), t_recv.at[0])
        for i in (2, 1, 3):
            pltpu.make_async_remote_copy(
                t_region(y), t_region(y), t_send.at[1], t_recv.at[1],
                device_id=y_device(i), device_id_type=MESH,
            ).start()

    def multiply(c):
        a = gath[c]
        for h in range(2):
            ob[c, h] = lax.dot_general(
                a, tg[h].reshape(NZ * block, tg.shape[4]),
                (((0,), (0,)), ((), ())), preferred_element_type=jnp.float32,
            )
            pltpu.make_async_remote_copy(
                ob.at[c, h], out.at[pl.ds(pl.multiple_of(hi * tile + c * kc, kc), kc), :],
                o_send, o_recv,
                device_id=(h * NZ + z, y, (1 - lo) * 2 + core), device_id_type=MESH,
            ).start()

    def forward(c, hop):
        for way in range(2):
            if hop:
                z_wait(c, way, hop - 1)
            z_send_hop(c, way, hop)

    wait_bytes(gath.at[:, rows_of(z, 0, rows), :], own_sem)
    forward(-WAVES, 0)
    scatter_early()
    for c in range(AHEAD):
        scatter_basis(c)
    for i in range(1, WAVES):
        wait_bytes(gath.at[:, rows_of(z, i * rows, rows), :], e_recv.at[i])
        forward(i - WAVES, 0)
    gather_targets_x()

    def finish(c):
        for way in range(2):
            z_wait(c, way, 3)
        multiply(c)

    def step(t, carry):
        pl.when(t >= TAIL)(lambda: finish(t - WHEN[4]))

        @pl.when(t < CHUNKS)
        def _():
            wait_bytes(gath.at[t, rows_of(z, WAVES * rows, block - WAVES * rows), :], x_recv.at[t])
            forward(t, 0)

        for hop in (1, 2, 3):
            c = t - WHEN[hop]
            for wave in range(-WAVES, 0):
                pl.when(c == wave)(lambda: forward(wave, hop))
            pl.when((c >= 0) & (c < CHUNKS))(lambda: forward(c, hop))

        pl.when(t == 1)(gather_targets_y)

        @pl.when(t + AHEAD < CHUNKS)
        def _():
            scatter_basis(t + AHEAD)

        c = t - WHEN[4]

        @pl.when(c == -1)
        def _():
            for way in range(2):
                for wave in range(-WAVES, 0):
                    z_wait(wave, way, 3)
            wait_bytes(tg.at[:, pl.ds(0, 6)], t_recv.at[1])

        @pl.when((c >= 0) & (t < TAIL))
        def _():
            finish(c)

        return carry

    lax.fori_loop(0, CHUNKS + WHEN[4], step, 0)

    wait_bytes(gath.at[:, pl.ds(0, block - rows), :], x_send)
    for way in range(2):
        wait_bytes(gath.at[:, pl.ds(0, 3 * block + block // 2), :], z_send.at[way])
    wait_bytes(tg.at[0, pl.ds(0, 4), pl.ds(0, NX - 1)], t_send.at[0])
    wait_bytes(tg.at[:, pl.ds(0, 6)], t_send.at[1])
    wait_bytes(ob, o_send)
    wait_bytes(out, o_recv)


def per_device(basis, targets):
    rows, columns = basis.shape[1:]
    samples, outs = targets.shape[1:]
    tile = columns // NX
    kc = tile // CHUNKS
    return pl.pallas_call(
        kernel,
        out_shape=jax.ShapeDtypeStruct((2 * tile, outs), jnp.float32),
        in_specs=[pl.BlockSpec(memory_space=pl.ANY)] * 2,
        out_specs=pl.BlockSpec(memory_space=pl.ANY),
        scratch_shapes=[
            pltpu.VMEM((CHUNKS, NZ * NX * rows, kc), jnp.bfloat16),
            pltpu.VMEM((2, NZ, NX, rows, outs), jnp.bfloat16),
            pltpu.VMEM((CHUNKS, 2, kc, outs), jnp.float32),
            pltpu.SemaphoreType.DMA,
            pltpu.SemaphoreType.DMA((WAVES,)),
            pltpu.SemaphoreType.DMA,
            pltpu.SemaphoreType.DMA((CHUNKS,)),
            pltpu.SemaphoreType.DMA((2,)),
            pltpu.SemaphoreType.DMA((2, CHUNKS + WAVES, 4)),
            pltpu.SemaphoreType.DMA((2,)),
            pltpu.SemaphoreType.DMA((2,)),
            pltpu.SemaphoreType.DMA,
            pltpu.SemaphoreType.DMA,
        ],
        compiler_params=pltpu.CompilerParams(
            collective_id=1, has_side_effects=True, vmem_limit_bytes=48 * 2**20
        ),
        name="cross",
    )(
        pltpu.with_memory_space_constraint(basis.reshape(rows, columns), pltpu.HBM),
        pltpu.with_memory_space_constraint(
            targets.reshape(samples // rows, rows, outs), pltpu.HBM
        ),
    )


def solution(mesh):
    in_specs = (P("depth", "row", "col"), P("depth", "col", "row"))
    out_specs = P(("col", "depth"), "row")
    return jax.shard_map(
        per_device, mesh=mesh, in_specs=in_specs, out_specs=out_specs, check_vma=False
    )
```
